32 devices in a mesh: row: 4 (over x, core), col: 8 (over z, y).
Axes of the slice: x: 2, y: 2, z: 4, core: 2. Of those that a mesh axis runs over, the one named last changes fastest.
Arguments:
- features: float32 [4096, 256], P(('row', 'col')), may hold values from -6 to 6
- adj_tiles: bfloat16 [4, 8, 96, 128, 128], P('row', 'col'), may hold values from 0 to 1, as said below
- tile_dst: int32 [4, 8, 96], P('row', 'col'), may hold values from 0 to 3, as said below
- tile_src: int32 [4, 8, 96], P('row', 'col'), may hold values from 0 to 7, as said below
- tile_count: int32 [4, 8], P('row', 'col'), may hold values from 1 to 96, as said below
- self_weight: float32 [256, 256], replicated, may hold values from -0.375 to 0.375
- neighbor_weight: float32 [256, 256], replicated, may hold values from -1.5 to 1.5
- layer_bias: float32 [256], replicated, may hold values from -3 to 3
Outputs:
- activated: float32 [4096, 256], P(('row', 'col'))
The draws below stay inside these ranges and needn't reach their ends.
Inputs may be any that keep to these rules, and one draw needn't show every extreme that they name: `adj_tiles`: every entry is 0 or 1. `tile_dst`: a destination tile within the column group of the device. `tile_src`: a source tile within the row group of the device. `tile_count`: list entries at and beyond a device's count are padding; every device holds at least one listed tile; some device holds exactly 96.
All inputs are finite; a program needn't handle non-finite values.
Results may differ from the reference program's by a relative error of at most 0.0003.
Values sent between devices are 32-bit elements; how exact they have to be, the bound alone decides.
No kernel may reach another device: no remote copies, remote signals or barrier semaphores. Data moves between devices by JAX's collectives and lax.ppermute only.
A program may use at most 64 MiB of HBM per device.

```python
import jax
import jax.numpy as jnp
from jax import lax

F = 256
F_OUT = 256
TILE = 128
NODE_DEV = 128
MAXT = 96
DST_TILES = 4
SRC_TILES = 8
NODES = 4096
N_ROW = 4
N_COL = 8


def draw_adj_tiles(key, part):
    linked = jax.random.bernoulli(key, 0.125, (N_ROW, N_COL, MAXT, TILE, TILE))
    return linked.astype(jnp.float32).astype(jnp.bfloat16)


def draw_tile_count(key, part):
    level = jax.random.randint(jax.random.fold_in(key, 1), (N_ROW, N_COL), 0, 4)
    jitter = jax.random.randint(jax.random.fold_in(key, 2), (N_ROW, N_COL), 0, MAXT // 8 + 1)
    counted = jnp.maximum(jnp.right_shift(jnp.int32(MAXT), level) - jitter, 1)
    chosen = jax.random.randint(jax.random.fold_in(key, 3), (), 0, N_ROW * N_COL)
    flat_counts = jnp.where(jnp.arange(N_ROW * N_COL) == chosen, MAXT, counted.reshape(-1))
    return flat_counts.reshape(N_ROW, N_COL).astype(jnp.int32)


def draw_tile_dst(key, part):
    raw_ids = jax.random.randint(jax.random.fold_in(key, 1), (N_ROW, N_COL, MAXT), 0, DST_TILES)
    isolated = jax.random.randint(jax.random.fold_in(key, 2), (N_COL,), 0, DST_TILES)
    flagged = jax.random.randint(jax.random.fold_in(key, 3), (N_COL,), 0, 2)
    struck = (raw_ids == isolated[None, :, None]) & (flagged[None, :, None] == 1)
    return jnp.where(struck, (raw_ids + 1) % DST_TILES, raw_ids).astype(jnp.int32)


def draw_tile_src(key, part):
    return jax.random.randint(key, (N_ROW, N_COL, MAXT), 0, SRC_TILES).astype(jnp.int32)


def level_of(own_key, shape, shards, low, top_value):
    gain, own = 1.0, jax.random.fold_in(own_key, 6)
    for position, parts in shards:
        draws = jnp.exp(jax.random.uniform(jax.random.fold_in(own, position), (parts,), jnp.float32, low / len(shards), top_value / len(shards)))
        gain = gain * jnp.repeat(draws, shape[position] // parts).reshape([-1 if axis == position else 1 for axis in range(len(shape))])
    return gain


def scatter_about(key, dims, width, reach, split=(), kind=jnp.bfloat16):
    entries = width * jax.random.normal(key, dims, jnp.float32)
    if split:
        entries = entries * level_of(key, dims, split, -0.22, 0.18)
    return jnp.clip(entries, -reach, reach).astype(kind)


def setup_inputs(seed: int = 0) -> dict:
    streams_of = jax.random.split(jax.random.key(seed), 9)
    features = scatter_about(streams_of[0], (NODES, F), 1.0, 6.0, ((0, 32),), jnp.float32)
    adj_tiles = draw_adj_tiles(jax.random.fold_in(streams_of[8], 71), 0)
    tile_dst = draw_tile_dst(jax.random.fold_in(streams_of[8], 71), 0)
    tile_src = draw_tile_src(jax.random.fold_in(streams_of[8], 71), 0)
    tile_count = draw_tile_count(jax.random.fold_in(streams_of[8], 71), 0)
    self_weight = scatter_about(streams_of[5], (F, F_OUT), F ** -0.5, 0.375, (), jnp.float32)
    neighbor_weight = scatter_about(streams_of[6], (F, F_OUT), 16 ** -0.5, 1.5, (), jnp.float32)
    layer_bias = scatter_about(streams_of[7], (F_OUT,), 0.5, 3.0, (), jnp.float32)
    return dict(features=features, adj_tiles=adj_tiles, tile_dst=tile_dst, tile_src=tile_src, tile_count=tile_count, self_weight=self_weight, neighbor_weight=neighbor_weight, layer_bias=layer_bias)


def reference(features, adj_tiles, tile_dst, tile_src, tile_count, self_weight, neighbor_weight, layer_bias):
    tiles_each = NODE_DEV // TILE
    tile_total = NODES // TILE
    devices_all = N_ROW * N_COL
    feature_tiles = features.reshape(tile_total, TILE, F)
    adjacency = adj_tiles.reshape(devices_all, MAXT, TILE, TILE)
    targets = tile_dst.reshape(devices_all, MAXT).astype(jnp.int32)
    sources = tile_src.reshape(devices_all, MAXT).astype(jnp.int32)
    counted = tile_count.reshape(devices_all).astype(jnp.int32)

    def visit(state_pair, entry):
        aggregate, degrees = state_pair
        device, blocks, target_ids, source_ids, valid_count = entry
        row_index = device // N_COL
        col_index = device % N_COL
        target_global = ((target_ids // tiles_each) * N_COL + col_index) * tiles_each + target_ids % tiles_each
        source_global = row_index * N_COL * tiles_each + source_ids
        live_slots = (jnp.arange(MAXT, dtype=jnp.int32) < valid_count).astype(jnp.float32)
        masked = blocks.astype(jnp.float32) * live_slots[:, None, None]
        products = jnp.einsum("kij,kjf->kif", masked, feature_tiles[source_global], precision=lax.Precision.HIGHEST)
        aggregate = aggregate.at[target_global].add(products)
        degrees = degrees.at[target_global].add(jnp.sum(masked, axis=2))
        return (aggregate, degrees), None

    start_pair = (jnp.zeros((tile_total, TILE, F), jnp.float32), jnp.zeros((tile_total, TILE), jnp.float32))
    (aggregate, degrees), _ = lax.scan(visit, start_pair, (jnp.arange(devices_all, dtype=jnp.int32), adjacency, targets, sources, counted))
    neighbor_mean = aggregate.reshape(NODES, F) / jnp.maximum(degrees.reshape(NODES), 1.0)[:, None]
    own_part = jnp.dot(features, self_weight, precision=lax.Precision.HIGHEST, preferred_element_type=jnp.float32)
    neighbor_part = jnp.dot(neighbor_mean, neighbor_weight, precision=lax.Precision.HIGHEST, preferred_element_type=jnp.float32)
    return jnp.maximum(own_part + neighbor_part + layer_bias, 0.0)
```

```python
import functools

import jax
import jax.numpy as jnp
from jax import lax
from jax.experimental import pallas as pl
from jax.experimental.pallas import tpu as pltpu
from jax.sharding import PartitionSpec as P

CHUNK = 8
PAD = 8
VMEM_BYTES = 48 * 1024 * 1024


def whole(space):
    return pl.BlockSpec(memory_space=space)


def split_bf16(value):
    high = value.astype(jnp.bfloat16)
    low = (value - high.astype(jnp.float32)).astype(jnp.bfloat16)
    return high, low


def matmul_f32(left, right):
    left_high, left_low = split_bf16(left)
    right_high, right_low = split_bf16(right)
    dot = functools.partial(jnp.dot, preferred_element_type=jnp.float32)
    return dot(left_high, right_high) + dot(left_high, right_low) + dot(left_low, right_high)


def combine_kernel(
    dst_ref, src_ref, count_ref, adj_ref, x_ref, ws_ref, b_ref,
    a_ref, deg_ref, own_ref, held, sems,
):
    maxt, tile = adj_ref.shape[0], adj_ref.shape[1]
    n_src, n_dst = a_ref.shape[0], a_ref.shape[1] // tile
    copies = []
    for first in range(0, maxt, CHUNK):
        part = pl.ds(first, CHUNK)
        copy = pltpu.make_async_copy(adj_ref.at[part], held.at[part], sems.at[first // CHUNK])
        copy.start()
        copies.append(copy)

    def clear(s, carry):
        a_ref[s] = jnp.zeros(a_ref.shape[1:], a_ref.dtype)
        return carry

    lax.fori_loop(0, n_src, clear, 0)
    own_ref[...] = matmul_f32(x_ref[...], ws_ref[...]) + b_ref[...]
    count = count_ref[0]

    def add_tile(k, carry):
        rows = pl.ds(pl.multiple_of(dst_ref[k] * tile, tile), tile)
        source = src_ref[k]
        a_ref[source, rows, :] = a_ref[source, rows, :] + held[k]
        return carry

    for index, copy in enumerate(copies):
        copy.wait()
        first = index * CHUNK
        lax.fori_loop(first, jnp.minimum(first + CHUNK, count), add_tile, 0)

    ones = jnp.ones((PAD, tile), jnp.bfloat16)

    def row_sums(d, carry):
        rows = pl.ds(pl.multiple_of(d * tile, tile), tile)

        def add_source(s, total):
            return total + lax.dot_general(
                ones, a_ref[s, rows, :], (((1,), (1,)), ((), ())),
                preferred_element_type=jnp.float32,
            )

        deg_ref[d] = lax.fori_loop(0, n_src, add_source, jnp.zeros((PAD, tile), jnp.float32))
        return carry

    lax.fori_loop(0, n_dst, row_sums, 0)


def combine(adj, dst, src, count, x, ws, b, n_src, n_dst):
    maxt, tile = adj.shape[0], adj.shape[1]
    return pl.pallas_call(
        combine_kernel,
        in_specs=[whole(pltpu.SMEM)] * 3 + [whole(pl.ANY)] + [whole(pltpu.VMEM)] * 3,
        out_specs=[whole(pltpu.VMEM)] * 3,
        out_shape=[
            jax.ShapeDtypeStruct((n_src, n_dst * tile, tile), jnp.bfloat16),
            jax.ShapeDtypeStruct((n_dst, PAD, tile), jnp.float32),
            jax.ShapeDtypeStruct((x.shape[0], ws.shape[1]), jnp.float32),
        ],
        scratch_shapes=[
            pltpu.VMEM(adj.shape, adj.dtype),
            pltpu.SemaphoreType.DMA((maxt // CHUNK,)),
        ],
        compiler_params=pltpu.CompilerParams(vmem_limit_bytes=VMEM_BYTES),
        name="combine_tiles",
    )(dst, src, count, adj, x, ws, b)


def product_rows(place_ref, a_ref, tile_refs, masks, halves, rows):
    total = None
    for index, mask in enumerate(masks):
        a = a_ref[place_ref[1] ^ mask, rows, :]
        term = jnp.dot(
            jnp.concatenate([a, a], axis=1), halves[index], preferred_element_type=jnp.float32
        )
        total = term if total is None else total + term
    return total


def stack_halves(tile_refs, halves):
    tile = tile_refs[0].shape[0]
    for index, ref in enumerate(tile_refs):
        high, low = split_bf16(ref[...])
        halves[index, 0:tile, :] = high
        halves[index, tile:, :] = low


def early_kernel(masks, place_ref, a_ref, *refs):
    tile_refs, acc_ref, halves = refs[: len(masks)], refs[-2], refs[-1]
    tile = tile_refs[0].shape[0]
    stack_halves(tile_refs, halves)

    def visit(d, carry):
        rows = pl.ds(pl.multiple_of(d * tile, tile), tile)
        acc_ref[rows, :] = product_rows(place_ref, a_ref, tile_refs, masks, halves, rows)
        return carry

    lax.fori_loop(0, acc_ref.shape[0] // tile, visit, 0)


def late_kernel(masks, place_ref, a_ref, deg_ref, acc_ref, *refs):
    tile_refs, out_refs, halves = refs[: len(masks)], refs[len(masks) : -1], refs[-1]
    tile, feat = tile_refs[0].shape
    stack_halves(tile_refs, halves)
    for step, out_ref in enumerate(out_refs):
        d = place_ref[0] ^ step
        rows = pl.ds(pl.multiple_of(d * tile, tile), tile)
        out_ref[0:tile, :] = acc_ref[rows, :] + product_rows(
            place_ref, a_ref, tile_refs, masks, halves, rows
        )
        out_ref[tile:, :] = jnp.concatenate([deg_ref[d]] * (feat // tile), axis=1)


def early(place, a, tiles, masks):
    tile, feat = tiles[0].shape
    return pl.pallas_call(
        functools.partial(early_kernel, masks),
        in_specs=[whole(pltpu.SMEM)] + [whole(pltpu.VMEM)] * (1 + len(tiles)),
        out_specs=whole(pltpu.VMEM),
        out_shape=jax.ShapeDtypeStruct((a.shape[1], feat), jnp.float32),
        scratch_shapes=[pltpu.VMEM((len(tiles), 2 * tile, feat), jnp.bfloat16)],
        compiler_params=pltpu.CompilerParams(vmem_limit_bytes=VMEM_BYTES),
        name="early_products",
    )(place, a, *tiles)


def late(place, a, deg, acc, tiles, masks, n_row):
    tile, feat = tiles[0].shape
    return pl.pallas_call(
        functools.partial(late_kernel, masks),
        in_specs=[whole(pltpu.SMEM)] + [whole(pltpu.VMEM)] * (3 + len(tiles)),
        out_specs=[whole(pltpu.VMEM)] * n_row,
        out_shape=[jax.ShapeDtypeStruct((tile + PAD, feat), jnp.float32)] * n_row,
        scratch_shapes=[pltpu.VMEM((len(tiles), 2 * tile, feat), jnp.bfloat16)],
        compiler_params=pltpu.CompilerParams(vmem_limit_bytes=VMEM_BYTES),
        name="late_products",
    )(place, a, deg, acc, *tiles)


def finish_kernel(own_ref, wn_ref, *refs):
    part_refs, out_ref = refs[:-1], refs[-1]
    tile = own_ref.shape[0]
    total = part_refs[0][...]
    for ref in part_refs[1:]:
        total = total + ref[...]
    degree = jnp.broadcast_to(total[tile : tile + 1, 0:tile], (tile, tile)).T
    degree = jnp.maximum(degree, 1.0)
    degree = jnp.concatenate([degree] * (total.shape[1] // tile), axis=1)
    mean = total[0:tile, :] / degree
    out_ref[...] = jnp.maximum(own_ref[...] + matmul_f32(mean, wn_ref[...]), 0.0)


def finish(own, wn, parts):
    return pl.pallas_call(
        finish_kernel,
        in_specs=[whole(pltpu.VMEM)] * (2 + len(parts)),
        out_specs=whole(pltpu.VMEM),
        out_shape=jax.ShapeDtypeStruct(own.shape, jnp.float32),
        compiler_params=pltpu.CompilerParams(vmem_limit_bytes=VMEM_BYTES),
        name="finish_rows",
    )(own, wn, *parts)


def exchange(value, axis, mask):
    pairs = [(i, i ^ mask) for i in range(lax.axis_size(axis))]
    return lax.ppermute(value, axis, pairs)


def on_device(
    features, adj_tiles, tile_dst, tile_src, tile_count, self_weight, neighbor_weight, layer_bias
):
    n_row, n_col = lax.axis_size("row"), lax.axis_size("col")
    tile = adj_tiles.shape[-1]
    assert features.shape[0] == tile and adj_tiles.shape[2] <= 256
    place = jnp.stack([lax.axis_index("row"), lax.axis_index("col")]).astype(jnp.int32)

    tiles = {0: features}
    bit = n_col // 2
    while bit:
        for mask in list(tiles):
            tiles[mask | bit] = exchange(tiles[mask], "col", bit)
        bit //= 2

    a, deg, own = combine(
        adj_tiles[0, 0], tile_dst[0, 0], tile_src[0, 0], tile_count[0], features,
        self_weight, layer_bias[None, :], n_col, n_row,
    )
    first = [m for m in tiles if m % 2 == 0]
    last = [m for m in tiles if m % 2 == 1]
    acc = early(place, a, [tiles[m] for m in first], first)
    parts = late(place, a, deg, acc, [tiles[m] for m in last], last, n_row)
    received = [parts[0]] + [exchange(parts[k], "row", k) for k in range(1, n_row)]
    return finish(own, neighbor_weight, received)


def solution(mesh):
    placed = (
        P(("row", "col"), None),
        P("row", "col", None, None, None),
        P("row", "col", None),
        P("row", "col", None),
        P("row", "col"),
        P(),
        P(),
        P(),
    )
    return jax.shard_map(
        on_device, mesh=mesh, in_specs=placed, out_specs=P(("row", "col"), None), check_vma=False
    )
```

```python
import functools

import jax
import jax.numpy as jnp
from jax import lax
from jax.experimental import pallas as pl
from jax.experimental.pallas import tpu as pltpu
from jax.sharding import PartitionSpec as P

CHUNK = 8
PAD = 8
VMEM_BYTES = 32 * 1024 * 1024
COMBINE_VMEM = 51 * 1024 * 1024


def whole(space):
    return pl.BlockSpec(memory_space=space)


def split_bf16(value):
    high = value.astype(jnp.bfloat16)
    low = (value - high.astype(jnp.float32)).astype(jnp.bfloat16)
    return high, low


def matmul_f32(left, right):
    left_high, left_low = split_bf16(left)
    right_high, right_low = split_bf16(right)
    dot = functools.partial(jnp.dot, preferred_element_type=jnp.float32)
    return dot(left_high, right_high) + dot(left_high, right_low) + dot(left_low, right_high)


def combine_kernel(lists_hbm, adj_hbm, a_ref, deg_ref, lists_ref, held, list_sem, sems):
    maxt, tile = held.shape[0], held.shape[1]
    n_src, n_dst = a_ref.shape[0], a_ref.shape[1] // tile
    lists = pltpu.make_async_copy(lists_hbm, lists_ref, list_sem)
    lists.start()
    blocks = []
    for first in range(0, maxt, CHUNK):
        part = pl.ds(first, CHUNK)
        copy = pltpu.make_async_copy(
            adj_hbm.at[0, 0, part], held.at[part], sems.at[first // CHUNK]
        )
        copy.start()
        blocks.append(copy)

    def clear(s, carry):
        a_ref[s] = jnp.zeros(a_ref.shape[1:], a_ref.dtype)
        return carry

    lax.fori_loop(0, n_src, clear, 0)
    lists.wait()
    count = lists_ref[2 * maxt]

    def add_tile(k, carry):
        rows = pl.ds(pl.multiple_of(lists_ref[k] * tile, tile), tile)
        source = lists_ref[maxt + k]
        a_ref[source, rows, :] = a_ref[source, rows, :] + held[k]
        return carry

    for index, copy in enumerate(blocks):
        copy.wait()
        first = index * CHUNK
        lax.fori_loop(first, jnp.minimum(first + CHUNK, count), add_tile, 0)

    ones = jnp.ones((PAD, tile), jnp.bfloat16)

    def row_sums(d, carry):
        rows = pl.ds(pl.multiple_of(d * tile, tile), tile)
        joined = lax.fori_loop(
            1, n_src, lambda s, total: total + a_ref[s, rows, :], a_ref[0, rows, :]
        )
        deg_ref[d] = lax.dot_general(
            ones, joined, (((1,), (1,)), ((), ())), preferred_element_type=jnp.float32
        )
        return carry

    lax.fori_loop(0, n_dst, row_sums, 0)


def combine(adj, dst, src, count, n_src, n_dst):
    maxt, tile = adj.shape[2], adj.shape[3]
    fill = -(2 * maxt + 1) % 128
    lists = jnp.concatenate([dst[0, 0], src[0, 0], count[0], jnp.zeros((fill,), jnp.int32)])
    return pl.pallas_call(
        combine_kernel,
        in_specs=[whole(pltpu.HBM)] * 2,
        out_specs=[whole(pltpu.VMEM)] * 2,
        out_shape=[
            jax.ShapeDtypeStruct((n_src, n_dst * tile, tile), jnp.bfloat16),
            jax.ShapeDtypeStruct((n_dst, PAD, tile), jnp.float32),
        ],
        scratch_shapes=[
            pltpu.SMEM(lists.shape, jnp.int32),
            pltpu.VMEM(adj.shape[2:], adj.dtype),
            pltpu.SemaphoreType.DMA(()),
            pltpu.SemaphoreType.DMA((maxt // CHUNK,)),
        ],
        compiler_params=pltpu.CompilerParams(vmem_limit_bytes=COMBINE_VMEM),
        name="combine_tiles",
    )(lists, adj)


def own_kernel(x_ref, ws_ref, b_ref, own_ref):
    own_ref[...] = matmul_f32(x_ref[...], ws_ref[...]) + b_ref[...][None, :]


def own_rows(x, ws, b):
    return pl.pallas_call(
        own_kernel,
        in_specs=[whole(pltpu.VMEM)] * 3,
        out_specs=whole(pltpu.VMEM),
        out_shape=jax.ShapeDtypeStruct((x.shape[0], ws.shape[1]), jnp.float32),
        compiler_params=pltpu.CompilerParams(vmem_limit_bytes=VMEM_BYTES),
        name="own_rows",
    )(x, ws, b)


def product_rows(a_ref, tile_refs, masks, halves, rows):
    total = None
    for index, mask in enumerate(masks):
        a = a_ref[lax.axis_index("col") ^ mask, rows, :]
        term = jnp.dot(
            jnp.concatenate([a, a], axis=1), halves[index], preferred_element_type=jnp.float32
        )
        total = term if total is None else total + term
    return total


def stack_halves(tile_refs, halves):
    tile = tile_refs[0].shape[0]
    for index, ref in enumerate(tile_refs):
        high, low = split_bf16(ref[...])
        halves[index, 0:tile, :] = high
        halves[index, tile:, :] = low


def early_kernel(masks, a_ref, *refs):
    tile_refs, acc_ref, halves = refs[: len(masks)], refs[-2], refs[-1]
    tile = tile_refs[0].shape[0]
    stack_halves(tile_refs, halves)

    def visit(d, carry):
        rows = pl.ds(pl.multiple_of(d * tile, tile), tile)
        acc_ref[rows, :] = product_rows(a_ref, tile_refs, masks, halves, rows)
        return carry

    lax.fori_loop(0, acc_ref.shape[0] // tile, visit, 0)


def late_kernel(masks, a_ref, deg_ref, acc_ref, *refs):
    tile_refs, out_refs, halves = refs[: len(masks)], refs[len(masks) : -1], refs[-1]
    tile, feat = tile_refs[0].shape
    stack_halves(tile_refs, halves)
    step = tile + PAD
    for index in range(acc_ref.shape[0] // tile):
        d = lax.axis_index("row") ^ index
        rows = pl.ds(pl.multiple_of(d * tile, tile), tile)
        out_ref, first = out_refs[index % 2], index // 2 * step
        out_ref[first : first + tile, :] = acc_ref[rows, :] + product_rows(
            a_ref, tile_refs, masks, halves, rows
        )
        out_ref[first + tile : first + step, :] = jnp.concatenate(
            [deg_ref[d]] * (feat // tile), axis=1
        )


def fold_kernel(step, keep_ref, came_ref, stay_ref, leave_ref):
    for index in range(keep_ref.shape[0] // step):
        out_ref, first = (stay_ref, leave_ref)[index % 2], index // 2 * step
        rows = slice(index * step, (index + 1) * step)
        out_ref[first : first + step, :] = keep_ref[rows, :] + came_ref[rows, :]


def fold(keep, came, step):
    half = jax.ShapeDtypeStruct((keep.shape[0] // 2, keep.shape[1]), jnp.float32)
    return pl.pallas_call(
        functools.partial(fold_kernel, step),
        in_specs=[whole(pltpu.VMEM)] * 2,
        out_specs=[whole(pltpu.VMEM)] * 2,
        out_shape=[half, half],
        compiler_params=pltpu.CompilerParams(vmem_limit_bytes=VMEM_BYTES),
        name="fold_sums",
    )(keep, came)


def early(a, tiles, masks):
    tile, feat = tiles[0].shape
    return pl.pallas_call(
        functools.partial(early_kernel, masks),
        in_specs=[whole(pltpu.VMEM)] * (1 + len(tiles)),
        out_specs=whole(pltpu.VMEM),
        out_shape=jax.ShapeDtypeStruct((a.shape[1], feat), jnp.float32),
        scratch_shapes=[pltpu.VMEM((len(tiles), 2 * tile, feat), jnp.bfloat16)],
        compiler_params=pltpu.CompilerParams(vmem_limit_bytes=VMEM_BYTES),
        name="early_products",
    )(a, *tiles)


def late(a, deg, acc, tiles, masks, n_row):
    tile, feat = tiles[0].shape
    return pl.pallas_call(
        functools.partial(late_kernel, masks),
        in_specs=[whole(pltpu.VMEM)] * (3 + len(tiles)),
        out_specs=[whole(pltpu.VMEM)] * 2,
        out_shape=[jax.ShapeDtypeStruct((n_row // 2 * (tile + PAD), feat), jnp.float32)] * 2,
        scratch_shapes=[pltpu.VMEM((len(tiles), 2 * tile, feat), jnp.bfloat16)],
        compiler_params=pltpu.CompilerParams(vmem_limit_bytes=VMEM_BYTES),
        name="late_products",
    )(a, deg, acc, *tiles)


def finish_kernel(own_ref, wn_ref, *refs):
    part_refs, out_ref = refs[:-1], refs[-1]
    tile = own_ref.shape[0]
    total = part_refs[0][...]
    for ref in part_refs[1:]:
        total = total + ref[...]
    degree = jnp.broadcast_to(total[tile : tile + 1, 0:tile], (tile, tile)).T
    degree = jnp.maximum(degree, 1.0)
    degree = jnp.concatenate([degree] * (total.shape[1] // tile), axis=1)
    mean = total[0:tile, :] / degree
    out_ref[...] = jnp.maximum(own_ref[...] + matmul_f32(mean, wn_ref[...]), 0.0)


def finish(own, wn, parts):
    return pl.pallas_call(
        finish_kernel,
        in_specs=[whole(pltpu.VMEM)] * (2 + len(parts)),
        out_specs=whole(pltpu.VMEM),
        out_shape=jax.ShapeDtypeStruct(own.shape, jnp.float32),
        compiler_params=pltpu.CompilerParams(vmem_limit_bytes=VMEM_BYTES),
        name="finish_rows",
    )(own, wn, *parts)


def exchange(value, axis, mask):
    pairs = [(i, i ^ mask) for i in range(lax.axis_size(axis))]
    return lax.ppermute(value, axis, pairs)


def on_device(
    features, adj_tiles, tile_dst, tile_src, tile_count, self_weight, neighbor_weight, layer_bias
):
    n_row, n_col = lax.axis_size("row"), lax.axis_size("col")
    tile = adj_tiles.shape[-1]
    assert features.shape[0] == tile and adj_tiles.shape[2] <= 256

    a, deg = combine(adj_tiles, tile_dst, tile_src, tile_count, n_col, n_row)
    tiles = {0: features}
    bits = [1 << k for k in reversed(range(1, n_col.bit_length() - 1))]
    for bit in bits:
        tiles[bit] = exchange(features, "col", bit)
    near = exchange(features, "col", 1)
    heads = [tiles[bit] for bit in bits]
    heads, a = lax.optimization_barrier((heads, a))
    tiles.update(zip(bits, heads))
    ready = [0] + bits
    for bit in bits:
        tiles[bit | 1] = exchange(tiles[bit], "col", 1)
    done = [0]
    for bit in bits:
        for mask in done[1:]:
            tiles[mask | bit] = exchange(tiles[mask], "col", bit)
        done = done + [mask | bit for mask in done]
    rest = [m for m in done if m not in ready]
    values = [tiles[m] for m in rest]
    values, near = lax.optimization_barrier((values, near))
    tiles[1] = near
    for mask, value in zip(rest, values):
        tiles[mask] = value
        tiles[mask | 1] = exchange(value, "col", 1)

    first = ready + [1]
    last = [m for m in tiles if m not in first]
    acc = early(a, [tiles[m] for m in first], first)
    own = own_rows(features, self_weight, layer_bias)
    keep, send = late(a, deg, acc, [tiles[m] for m in last], last, n_row)
    bit = 1
    while 2 * bit < n_row:
        keep, send = fold(keep, exchange(send, "row", bit), tile + PAD)
        bit *= 2
    return finish(own, neighbor_weight, [keep, exchange(send, "row", bit)])


def solution(mesh):
    placed = (
        P(("row", "col"), None),
        P("row", "col", None, None, None),
        P("row", "col", None),
        P("row", "col", None),
        P("row", "col"),
        P(),
        P(),
        P(),
    )
    return jax.shard_map(
        on_device, mesh=mesh, in_specs=placed, out_specs=P(("row", "col"), None), check_vma=False
    )
```

```python
import functools

import jax
import jax.numpy as jnp
from jax import lax
from jax.experimental import pallas as pl
from jax.experimental.pallas import tpu as pltpu
from jax.sharding import PartitionSpec as P

CHUNK = 8
PAD = 8
VMEM_BYTES = 32 * 1024 * 1024
COMBINE_VMEM = 51 * 1024 * 1024


def whole(space):
    return pl.BlockSpec(memory_space=space)


def split_bf16(value):
    high = value.astype(jnp.bfloat16)
    low = (value - high.astype(jnp.float32)).astype(jnp.bfloat16)
    return high, low


def matmul_f32(left, right):
    left_high, left_low = split_bf16(left)
    right_high, right_low = split_bf16(right)
    dot = functools.partial(jnp.dot, preferred_element_type=jnp.float32)
    return dot(left_high, right_high) + dot(left_high, right_low) + dot(left_low, right_high)


def combine_kernel(lists_hbm, adj_hbm, a_ref, deg_ref, lists_ref, held, list_sem, sems):
    maxt, tile = held.shape[0], held.shape[1]
    n_src, n_dst = a_ref.shape[0], a_ref.shape[1] // tile
    lists = pltpu.make_async_copy(lists_hbm, lists_ref, list_sem)
    lists.start()
    blocks = []
    for first in range(0, maxt, CHUNK):
        part = pl.ds(first, CHUNK)
        copy = pltpu.make_async_copy(
            adj_hbm.at[0, 0, part], held.at[part], sems.at[first // CHUNK]
        )
        copy.start()
        blocks.append(copy)

    def clear(s, carry):
        a_ref[s] = jnp.zeros(a_ref.shape[1:], a_ref.dtype)
        return carry

    lax.fori_loop(0, n_src, clear, 0)
    lists.wait()
    count = lists_ref[2 * maxt]

    def add_tile(k, carry):
        rows = pl.ds(pl.multiple_of(lists_ref[k] * tile, tile), tile)
        source = lists_ref[maxt + k]
        a_ref[source, rows, :] = a_ref[source, rows, :] + held[k]
        return carry

    for index, copy in enumerate(blocks):
        copy.wait()
        first = index * CHUNK
        lax.fori_loop(first, jnp.minimum(first + CHUNK, count), add_tile, 0)

    ones = jnp.ones((PAD, tile), jnp.bfloat16)

    def row_sums(d, carry):
        rows = pl.ds(pl.multiple_of(d * tile, tile), tile)
        joined = lax.fori_loop(
            1, n_src, lambda s, total: total + a_ref[s, rows, :], a_ref[0, rows, :]
        )
        deg_ref[d] = lax.dot_general(
            ones, joined, (((1,), (1,)), ((), ())), preferred_element_type=jnp.float32
        )
        return carry

    lax.fori_loop(0, n_dst, row_sums, 0)


def combine(adj, lists, n_src, n_dst):
    maxt, tile = adj.shape[2], adj.shape[3]
    return pl.pallas_call(
        combine_kernel,
        in_specs=[whole(pltpu.HBM)] * 2,
        out_specs=[whole(pltpu.VMEM)] * 2,
        out_shape=[
            jax.ShapeDtypeStruct((n_src, n_dst * tile, tile), jnp.bfloat16),
            jax.ShapeDtypeStruct((n_dst, PAD, tile), jnp.float32),
        ],
        scratch_shapes=[
            pltpu.SMEM(lists.shape, jnp.int32),
            pltpu.VMEM(adj.shape[2:], adj.dtype),
            pltpu.SemaphoreType.DMA(()),
            pltpu.SemaphoreType.DMA((maxt // CHUNK,)),
        ],
        compiler_params=pltpu.CompilerParams(vmem_limit_bytes=COMBINE_VMEM),
        name="combine_tiles",
    )(lists, adj)


def own_kernel(x_ref, ws_ref, b_ref, own_ref):
    own_ref[...] = matmul_f32(x_ref[...], ws_ref[...]) + b_ref[...][None, :]


def own_rows(x, ws, b):
    return pl.pallas_call(
        own_kernel,
        in_specs=[whole(pltpu.VMEM)] * 3,
        out_specs=whole(pltpu.VMEM),
        out_shape=jax.ShapeDtypeStruct((x.shape[0], ws.shape[1]), jnp.float32),
        compiler_params=pltpu.CompilerParams(vmem_limit_bytes=VMEM_BYTES),
        name="own_rows",
    )(x, ws, b)


def product_rows(a_ref, tile_refs, masks, halves, rows):
    total = None
    for index, mask in enumerate(masks):
        a = a_ref[lax.axis_index("col") ^ mask, rows, :]
        term = jnp.dot(
            jnp.concatenate([a, a], axis=1), halves[index], preferred_element_type=jnp.float32
        )
        total = term if total is None else total + term
    return total


def stack_halves(tile_refs, halves):
    tile = tile_refs[0].shape[0]
    for index, ref in enumerate(tile_refs):
        high, low = split_bf16(ref[...])
        halves[index, 0:tile, :] = high
        halves[index, tile:, :] = low


def early_kernel(masks, a_ref, *refs):
    tile_refs, acc_ref, halves = refs[: len(masks)], refs[-2], refs[-1]
    tile = tile_refs[0].shape[0]
    stack_halves(tile_refs, halves)

    def visit(d, carry):
        rows = pl.ds(pl.multiple_of(d * tile, tile), tile)
        acc_ref[rows, :] = product_rows(a_ref, tile_refs, masks, halves, rows)
        return carry

    lax.fori_loop(0, acc_ref.shape[0] // tile, visit, 0)


def late_kernel(masks, a_ref, deg_ref, acc_ref, *refs):
    tile_refs, out_refs, halves = refs[: len(masks)], refs[len(masks) : -1], refs[-1]
    tile, feat = tile_refs[0].shape
    stack_halves(tile_refs, halves)
    step = tile + PAD
    for index in range(acc_ref.shape[0] // tile):
        d = lax.axis_index("row") ^ index
        rows = pl.ds(pl.multiple_of(d * tile, tile), tile)
        out_ref, first = out_refs[index % 2], index // 2 * step
        out_ref[first : first + tile, :] = acc_ref[rows, :] + product_rows(
            a_ref, tile_refs, masks, halves, rows
        )
        out_ref[first + tile : first + step, :] = jnp.concatenate(
            [deg_ref[d]] * (feat // tile), axis=1
        )


def fold_kernel(step, keep_ref, came_ref, stay_ref, leave_ref):
    for index in range(keep_ref.shape[0] // step):
        out_ref, first = (stay_ref, leave_ref)[index % 2], index // 2 * step
        rows = slice(index * step, (index + 1) * step)
        out_ref[first : first + step, :] = keep_ref[rows, :] + came_ref[rows, :]


def fold(keep, came, step):
    half = jax.ShapeDtypeStruct((keep.shape[0] // 2, keep.shape[1]), jnp.float32)
    return pl.pallas_call(
        functools.partial(fold_kernel, step),
        in_specs=[whole(pltpu.VMEM)] * 2,
        out_specs=[whole(pltpu.VMEM)] * 2,
        out_shape=[half, half],
        compiler_params=pltpu.CompilerParams(vmem_limit_bytes=VMEM_BYTES),
        name="fold_sums",
    )(keep, came)


def early(a, tiles, masks):
    tile, feat = tiles[0].shape
    return pl.pallas_call(
        functools.partial(early_kernel, masks),
        in_specs=[whole(pltpu.VMEM)] * (1 + len(tiles)),
        out_specs=whole(pltpu.VMEM),
        out_shape=jax.ShapeDtypeStruct((a.shape[1], feat), jnp.float32),
        scratch_shapes=[pltpu.VMEM((len(tiles), 2 * tile, feat), jnp.bfloat16)],
        compiler_params=pltpu.CompilerParams(vmem_limit_bytes=VMEM_BYTES),
        name="early_products",
    )(a, *tiles)


def late(a, deg, acc, tiles, masks, n_row):
    tile, feat = tiles[0].shape
    return pl.pallas_call(
        functools.partial(late_kernel, masks),
        in_specs=[whole(pltpu.VMEM)] * (3 + len(tiles)),
        out_specs=[whole(pltpu.VMEM)] * 2,
        out_shape=[jax.ShapeDtypeStruct((n_row // 2 * (tile + PAD), feat), jnp.float32)] * 2,
        scratch_shapes=[pltpu.VMEM((len(tiles), 2 * tile, feat), jnp.bfloat16)],
        compiler_params=pltpu.CompilerParams(vmem_limit_bytes=VMEM_BYTES),
        name="late_products",
    )(a, deg, acc, *tiles)


def finish_kernel(own_ref, wn_ref, *refs):
    part_refs, out_ref = refs[:-1], refs[-1]
    tile = own_ref.shape[0]
    total = part_refs[0][...]
    for ref in part_refs[1:]:
        total = total + ref[...]
    degree = jnp.broadcast_to(total[tile : tile + 1, 0:tile], (tile, tile)).T
    degree = jnp.maximum(degree, 1.0)
    degree = jnp.concatenate([degree] * (total.shape[1] // tile), axis=1)
    mean = total[0:tile, :] / degree
    out_ref[...] = jnp.maximum(own_ref[...] + matmul_f32(mean, wn_ref[...]), 0.0)


def finish(own, wn, parts):
    return pl.pallas_call(
        finish_kernel,
        in_specs=[whole(pltpu.VMEM)] * (2 + len(parts)),
        out_specs=whole(pltpu.VMEM),
        out_shape=jax.ShapeDtypeStruct(own.shape, jnp.float32),
        compiler_params=pltpu.CompilerParams(vmem_limit_bytes=VMEM_BYTES),
        name="finish_rows",
    )(own, wn, *parts)


def after(value, *earlier):
    return lax.optimization_barrier((value, *earlier))[0]


def exchange(value, axis, mask):
    pairs = [(i, i ^ mask) for i in range(lax.axis_size(axis))]
    return lax.ppermute(value, axis, pairs)


def on_device(
    features, adj_tiles, tile_dst, tile_src, tile_count, self_weight, neighbor_weight, layer_bias
):
    n_row, n_col = lax.axis_size("row"), lax.axis_size("col")
    tile = adj_tiles.shape[-1]
    assert features.shape[0] == tile and adj_tiles.shape[2] <= 256

    bits = [1 << k for k in reversed(range(1, n_col.bit_length() - 1))]
    tiles = {0: features}
    across = n_col - 1
    for mask in bits + [1, across]:
        tiles[mask] = exchange(features, "col", mask)
    fill = -(2 * tile_dst.shape[2] + 1) % 128
    lists = jnp.concatenate(
        [tile_dst[0, 0], tile_src[0, 0], tile_count[0], jnp.zeros((fill,), jnp.int32)]
    )
    tiles[bits[0]], lists = lax.optimization_barrier((tiles[bits[0]], lists))

    for mask in range(2, n_col):
        top = 1 << (mask.bit_length() - 1)
        if mask in tiles:
            continue
        if mask % 2:
            tiles[mask] = exchange(tiles[mask ^ 1], "col", 1)
        else:
            tiles[mask] = exchange(tiles[top], "col", mask ^ top)
    a, deg = combine(adj_tiles, lists, n_col, n_row)
    first = [0, 1] + bits + [across]
    last = [m for m in tiles if m not in first]
    acc = early(a, [tiles[m] for m in first], first)
    own = own_rows(features, self_weight, layer_bias)
    keep, send = late(a, deg, acc, [tiles[m] for m in last], last, n_row)
    bit = 1
    while 2 * bit < n_row:
        keep, send = fold(keep, exchange(send, "row", bit), tile + PAD)
        bit *= 2
    return finish(own, neighbor_weight, [keep, exchange(send, "row", bit)])


def solution(mesh):
    placed = (
        P(("row", "col"), None),
        P("row", "col", None, None, None),
        P("row", "col", None),
        P("row", "col", None),
        P("row", "col"),
        P(),
        P(),
        P(),
    )
    return jax.shard_map(
        on_device, mesh=mesh, in_specs=placed, out_specs=P(("row", "col"), None), check_vma=False
    )
```

```python
import functools

import jax
import jax.numpy as jnp
from jax import lax
from jax.experimental import pallas as pl
from jax.experimental.pallas import tpu as pltpu
from jax.sharding import PartitionSpec as P

CHUNK = 8
PAD = 8
EAGER = 4
VMEM_BYTES = 32 * 1024 * 1024
COMBINE_VMEM = 51 * 1024 * 1024


def whole(space):
    return pl.BlockSpec(memory_space=space)


def split_bf16(value):
    high = value.astype(jnp.bfloat16)
    low = (value - high.astype(jnp.float32)).astype(jnp.bfloat16)
    return high, low


def matmul_f32(left, right):
    left_high, left_low = split_bf16(left)
    right_high, right_low = split_bf16(right)
    dot = functools.partial(jnp.dot, preferred_element_type=jnp.float32)
    return dot(left_high, right_high) + dot(left_high, right_low) + dot(left_low, right_high)


def combine_kernel(lists_hbm, adj_hbm, a_ref, deg_ref, lists_ref, held, list_sem, sems):
    maxt, tile = held.shape[0], held.shape[1]
    n_src, n_dst = a_ref.shape[0], a_ref.shape[1] // tile
    lists = pltpu.make_async_copy(lists_hbm, lists_ref, list_sem)
    lists.start()

    def block(index):
        part = pl.ds(index * CHUNK, CHUNK)
        return pltpu.make_async_copy(adj_hbm.at[0, 0, part], held.at[part], sems.at[index])

    chunks = maxt // CHUNK
    ahead = min(EAGER, chunks)
    for index in range(ahead):
        block(index).start()

    def clear(s, carry):
        a_ref[s] = jnp.zeros(a_ref.shape[1:], a_ref.dtype)
        return carry

    lax.fori_loop(0, n_src, clear, 0)
    lists.wait()
    count = lists_ref[2 * maxt]

    for index in range(ahead, chunks):

        @pl.when(index * CHUNK < count)
        def _():
            block(index).start()

    def add_tile(k, carry):
        rows = pl.ds(pl.multiple_of(lists_ref[k] * tile, tile), tile)
        source = lists_ref[maxt + k]
        a_ref[source, rows, :] = a_ref[source, rows, :] + held[k]
        return carry

    def add_block(index):
        block(index).wait()
        first = index * CHUNK
        lax.fori_loop(first, jnp.minimum(first + CHUNK, count), add_tile, 0)

    for index in range(chunks):
        if index < ahead:
            add_block(index)
        else:
            pl.when(index * CHUNK < count)(functools.partial(add_block, index))

    ones = jnp.ones((PAD, tile), jnp.bfloat16)

    def row_sums(d, carry):
        rows = pl.ds(pl.multiple_of(d * tile, tile), tile)
        joined = lax.fori_loop(
            1, n_src, lambda s, total: total + a_ref[s, rows, :], a_ref[0, rows, :]
        )
        deg_ref[d] = lax.dot_general(
            ones, joined, (((1,), (1,)), ((), ())), preferred_element_type=jnp.float32
        )
        return carry

    lax.fori_loop(0, n_dst, row_sums, 0)


def combine(adj, lists, n_src, n_dst):
    maxt, tile = adj.shape[2], adj.shape[3]
    return pl.pallas_call(
        combine_kernel,
        in_specs=[whole(pltpu.HBM)] * 2,
        out_specs=[whole(pltpu.VMEM)] * 2,
        out_shape=[
            jax.ShapeDtypeStruct((n_src, n_dst * tile, tile), jnp.bfloat16),
            jax.ShapeDtypeStruct((n_dst, PAD, tile), jnp.float32),
        ],
        scratch_shapes=[
            pltpu.SMEM(lists.shape, jnp.int32),
            pltpu.VMEM(adj.shape[2:], adj.dtype),
            pltpu.SemaphoreType.DMA(()),
            pltpu.SemaphoreType.DMA((maxt // CHUNK,)),
        ],
        compiler_params=pltpu.CompilerParams(vmem_limit_bytes=COMBINE_VMEM),
        name="combine_tiles",
    )(lists, adj)


def own_kernel(x_ref, ws_ref, b_ref, own_ref):
    own_ref[...] = matmul_f32(x_ref[...], ws_ref[...]) + b_ref[...][None, :]


def own_rows(x, ws, b):
    return pl.pallas_call(
        own_kernel,
        in_specs=[whole(pltpu.VMEM)] * 3,
        out_specs=whole(pltpu.VMEM),
        out_shape=jax.ShapeDtypeStruct((x.shape[0], ws.shape[1]), jnp.float32),
        compiler_params=pltpu.CompilerParams(vmem_limit_bytes=VMEM_BYTES),
        name="own_rows",
    )(x, ws, b)


def by_core(pair):
    return pair[0] + lax.rem(lax.axis_index("row"), 2) * (pair[1] - pair[0])


def product_rows(a_ref, tile_refs, masks, halves, rows):
    total = None
    for index, mask in enumerate(masks):
        a = a_ref[lax.axis_index("col") ^ by_core(mask), rows, :]
        term = jnp.dot(
            jnp.concatenate([a, a], axis=1), halves[index], preferred_element_type=jnp.float32
        )
        total = term if total is None else total + term
    return total


def stack_halves(tile_refs, halves):
    tile = tile_refs[0].shape[0]
    for index, ref in enumerate(tile_refs):
        high, low = split_bf16(ref[...])
        halves[index, 0:tile, :] = high
        halves[index, tile:, :] = low


def early_kernel(masks, a_ref, *refs):
    tile_refs, acc_ref, halves = refs[: len(masks)], refs[-2], refs[-1]
    stack_halves(tile_refs, halves)
    height = min(acc_ref.shape[0], 512)

    def visit(step, carry):
        rows = pl.ds(pl.multiple_of(step * height, height), height)
        acc_ref[rows, :] = product_rows(a_ref, tile_refs, masks, halves, rows)
        return carry

    lax.fori_loop(0, acc_ref.shape[0] // height, visit, 0)


def late_kernel(masks, a_ref, deg_ref, acc_ref, *refs):
    tile_refs, out_refs, halves = refs[: len(masks)], refs[len(masks) : -1], refs[-1]
    tile, feat = tile_refs[0].shape
    stack_halves(tile_refs, halves)
    for index, out_ref in enumerate(out_refs):
        d = lax.axis_index("row") ^ index
        rows = pl.ds(pl.multiple_of(d * tile, tile), tile)
        out_ref[0:tile, :] = acc_ref[rows, :] + product_rows(
            a_ref, tile_refs, masks, halves, rows
        )
        out_ref[tile:, :] = jnp.concatenate([deg_ref[d]] * (feat // tile), axis=1)


def fold_kernel(keep_ref, came_ref, out_ref):
    out_ref[...] = keep_ref[...] + came_ref[...]


def fold(keep, came):
    return pl.pallas_call(
        fold_kernel,
        in_specs=[whole(pltpu.VMEM)] * 2,
        out_specs=whole(pltpu.VMEM),
        out_shape=jax.ShapeDtypeStruct(keep.shape, jnp.float32),
        compiler_params=pltpu.CompilerParams(vmem_limit_bytes=VMEM_BYTES),
        name="fold_sums",
    )(keep, came)


def early(a, tiles, masks):
    tile, feat = tiles[0].shape
    return pl.pallas_call(
        functools.partial(early_kernel, masks),
        in_specs=[whole(pltpu.VMEM)] * (1 + len(tiles)),
        out_specs=whole(pltpu.VMEM),
        out_shape=jax.ShapeDtypeStruct((a.shape[1], feat), jnp.float32),
        scratch_shapes=[pltpu.VMEM((len(tiles), 2 * tile, feat), jnp.bfloat16)],
        compiler_params=pltpu.CompilerParams(vmem_limit_bytes=VMEM_BYTES),
        name="early_products",
    )(a, *tiles)


def late(a, deg, acc, tiles, masks, n_row):
    tile, feat = tiles[0].shape
    return pl.pallas_call(
        functools.partial(late_kernel, masks),
        in_specs=[whole(pltpu.VMEM)] * (3 + len(tiles)),
        out_specs=[whole(pltpu.VMEM)] * n_row,
        out_shape=[jax.ShapeDtypeStruct((tile + PAD, feat), jnp.float32)] * n_row,
        scratch_shapes=[pltpu.VMEM((len(tiles), 2 * tile, feat), jnp.bfloat16)],
        compiler_params=pltpu.CompilerParams(vmem_limit_bytes=VMEM_BYTES),
        name="late_products",
    )(a, deg, acc, *tiles)


def finish_kernel(own_ref, wn_ref, *refs):
    part_refs, out_ref = refs[:-1], refs[-1]
    tile, width = own_ref.shape
    total = part_refs[0][...]
    for ref in part_refs[1:]:
        total = total + ref[...]
    degree = jnp.broadcast_to(total[tile : tile + 1, 0:tile], (tile, tile)).T
    scale = 1.0 / jnp.maximum(degree, 1.0)
    scale = jnp.concatenate([scale] * (width // tile), axis=1)
    product = matmul_f32(total[0:tile, :], wn_ref[...])
    out_ref[...] = jnp.maximum(own_ref[...] + product * scale, 0.0)


def finish(own, wn, parts):
    return pl.pallas_call(
        finish_kernel,
        in_specs=[whole(pltpu.VMEM)] * (2 + len(parts)),
        out_specs=whole(pltpu.VMEM),
        out_shape=jax.ShapeDtypeStruct(own.shape, jnp.float32),
        compiler_params=pltpu.CompilerParams(vmem_limit_bytes=VMEM_BYTES),
        name="finish_rows",
    )(own, wn, *parts)


def after(value, *earlier):
    return lax.optimization_barrier((value, *earlier))[0]


def swap(value, pair):
    n_row, n_col = lax.axis_size("row"), lax.axis_size("col")
    pairs = [
        (r * n_col + c, r * n_col + (c ^ pair[r % 2])) for r in range(n_row) for c in range(n_col)
    ]
    return lax.ppermute(value, ("row", "col"), pairs)


def exchange(value, axis, mask):
    pairs = [(i, i ^ mask) for i in range(lax.axis_size(axis))]
    return lax.ppermute(value, axis, pairs)


def on_device(
    features, adj_tiles, tile_dst, tile_src, tile_count, self_weight, neighbor_weight, layer_bias
):
    n_row, n_col = lax.axis_size("row"), lax.axis_size("col")
    tile, maxt = adj_tiles.shape[-1], adj_tiles.shape[2]
    assert features.shape[0] == tile and maxt <= 256
    fill = -(2 * maxt + 1) % 128
    lists = jnp.concatenate(
        [tile_dst[0, 0], tile_src[0, 0], tile_count[0], jnp.zeros((fill,), jnp.int32)]
    )

    half = n_col // 2
    middle = list(range(3, half))
    pairs = [(half, half)] + list(zip([1] + middle + [2], [2] + middle + [1]))
    tiles = {pair: swap(features, pair) for pair in pairs}
    tiles[0, 0] = features
    first = list(tiles)
    far, lists = lax.optimization_barrier((tiles[half, half], lists))
    a, deg = combine(adj_tiles, lists, n_col, n_row)
    for mask in reversed(range(1, half)):
        tiles[half + mask, half + mask] = swap(far, (mask, mask))
    last = [pair for pair in tiles if pair not in first]
    acc = early(a, [tiles[pair] for pair in first], first)
    own = own_rows(features, self_weight, layer_bias)

    blocks = late(a, deg, acc, [tiles[pair] for pair in last], last, n_row)
    while len(blocks) > 4:
        bit = len(blocks) // 2
        blocks = [fold(blocks[m], exchange(blocks[m | bit], "row", bit)) for m in range(bit)]
    own_sum, beside, across, both = blocks
    across = exchange(fold(across, exchange(both, "row", 1)), "row", 2)
    beside = after(exchange(beside, "row", 1), across)
    return finish(own, neighbor_weight, [own_sum, beside, across])


def solution(mesh):
    placed = (
        P(("row", "col"), None),
        P("row", "col", None, None, None),
        P("row", "col", None),
        P("row", "col", None),
        P("row", "col"),
        P(),
        P(),
        P(),
    )
    return jax.shard_map(
        on_device, mesh=mesh, in_specs=placed, out_specs=P(("row", "col"), None), check_vma=False
    )
```

```python
import functools

import jax
import jax.numpy as jnp
from jax import lax
from jax.experimental import pallas as pl
from jax.experimental.pallas import tpu as pltpu
from jax.sharding import PartitionSpec as P

CHUNK = 8
PAD = 8
EAGER = 4
VMEM_BYTES = 32 * 1024 * 1024
COMBINE_VMEM = 51 * 1024 * 1024


def whole(space):
    return pl.BlockSpec(memory_space=space)


def split_bf16(value):
    high = value.astype(jnp.bfloat16)
    low = (value - high.astype(jnp.float32)).astype(jnp.bfloat16)
    return high, low


def matmul_f32(left, right):
    left_high, left_low = split_bf16(left)
    right_high, right_low = split_bf16(right)
    dot = functools.partial(jnp.dot, preferred_element_type=jnp.float32)
    return dot(left_high, right_high) + dot(left_high, right_low) + dot(left_low, right_high)


def combine_kernel(lists_hbm, adj_hbm, a_ref, deg_ref, lists_ref, held, list_sem, sems):
    maxt, tile = held.shape[0], held.shape[1]
    n_src, n_dst = a_ref.shape[0], a_ref.shape[1] // tile
    lists = pltpu.make_async_copy(lists_hbm, lists_ref, list_sem)
    lists.start()

    def block(index):
        part = pl.ds(index * CHUNK, CHUNK)
        return pltpu.make_async_copy(adj_hbm.at[0, 0, part], held.at[part], sems.at[index])

    chunks = maxt // CHUNK
    ahead = min(EAGER, chunks)
    for index in range(ahead):
        block(index).start()

    def clear(s, carry):
        a_ref[s] = jnp.zeros(a_ref.shape[1:], a_ref.dtype)
        return carry

    lax.fori_loop(0, n_src, clear, 0)
    lists.wait()
    count = lists_ref[2 * maxt]

    for index in range(ahead, chunks):

        @pl.when(index * CHUNK < count)
        def _():
            block(index).start()

    def add_tile(k, carry):
        rows = pl.ds(pl.multiple_of(lists_ref[k] * tile, tile), tile)
        source = lists_ref[maxt + k]
        a_ref[source, rows, :] = a_ref[source, rows, :] + held[k]
        return carry

    def add_block(index):
        block(index).wait()
        first = index * CHUNK
        lax.fori_loop(first, jnp.minimum(first + CHUNK, count), add_tile, 0)

    for index in range(chunks):
        if index < ahead:
            add_block(index)
        else:
            pl.when(index * CHUNK < count)(functools.partial(add_block, index))

    ones = jnp.ones((PAD, tile), jnp.bfloat16)

    def row_sums(d, carry):
        rows = pl.ds(pl.multiple_of(d * tile, tile), tile)
        joined = lax.fori_loop(
            1, n_src, lambda s, total: total + a_ref[s, rows, :], a_ref[0, rows, :]
        )
        deg_ref[d] = lax.dot_general(
            ones, joined, (((1,), (1,)), ((), ())), preferred_element_type=jnp.float32
        )
        return carry

    lax.fori_loop(0, n_dst, row_sums, 0)


def combine(adj, lists, n_src, n_dst):
    maxt, tile = adj.shape[2], adj.shape[3]
    return pl.pallas_call(
        combine_kernel,
        in_specs=[whole(pltpu.HBM)] * 2,
        out_specs=[whole(pltpu.VMEM)] * 2,
        out_shape=[
            jax.ShapeDtypeStruct((n_src, n_dst * tile, tile), jnp.bfloat16),
            jax.ShapeDtypeStruct((n_dst, PAD, tile), jnp.float32),
        ],
        scratch_shapes=[
            pltpu.SMEM(lists.shape, jnp.int32),
            pltpu.VMEM(adj.shape[2:], adj.dtype),
            pltpu.SemaphoreType.DMA(()),
            pltpu.SemaphoreType.DMA((maxt // CHUNK,)),
        ],
        compiler_params=pltpu.CompilerParams(vmem_limit_bytes=COMBINE_VMEM),
        name="combine_tiles",
    )(lists, adj)


def own_kernel(x_ref, ws_ref, b_ref, own_ref):
    own_ref[...] = matmul_f32(x_ref[...], ws_ref[...]) + b_ref[...][None, :]


def own_rows(x, ws, b):
    return pl.pallas_call(
        own_kernel,
        in_specs=[whole(pltpu.VMEM)] * 3,
        out_specs=whole(pltpu.VMEM),
        out_shape=jax.ShapeDtypeStruct((x.shape[0], ws.shape[1]), jnp.float32),
        compiler_params=pltpu.CompilerParams(vmem_limit_bytes=VMEM_BYTES),
        name="own_rows",
    )(x, ws, b)


def product_rows(a_ref, tile_refs, masks, halves, rows):
    total = None
    for index, mask in enumerate(masks):
        a = a_ref[lax.axis_index("col") ^ mask, rows, :]
        term = jnp.dot(
            jnp.concatenate([a, a], axis=1), halves[index], preferred_element_type=jnp.float32
        )
        total = term if total is None else total + term
    return total


def stack_halves(tile_refs, halves):
    tile = tile_refs[0].shape[0]
    for index, ref in enumerate(tile_refs):
        high, low = split_bf16(ref[...])
        halves[index, 0:tile, :] = high
        halves[index, tile:, :] = low


def early_kernel(masks, a_ref, *refs):
    tile_refs, acc_ref, halves = refs[: len(masks)], refs[-2], refs[-1]
    stack_halves(tile_refs, halves)
    height = min(acc_ref.shape[0], 512)

    def visit(step, carry):
        rows = pl.ds(pl.multiple_of(step * height, height), height)
        acc_ref[rows, :] = product_rows(a_ref, tile_refs, masks, halves, rows)
        return carry

    lax.fori_loop(0, acc_ref.shape[0] // height, visit, 0)


def late_kernel(masks, a_ref, deg_ref, acc_ref, *refs):
    tile_refs, out_refs, halves = refs[: len(masks)], refs[len(masks) : -1], refs[-1]
    tile, feat = tile_refs[0].shape
    stack_halves(tile_refs, halves)
    for index, out_ref in enumerate(out_refs):
        d = lax.axis_index("row") ^ index
        rows = pl.ds(pl.multiple_of(d * tile, tile), tile)
        out_ref[0:tile, :] = acc_ref[rows, :] + product_rows(
            a_ref, tile_refs, masks, halves, rows
        )
        out_ref[tile:, :] = jnp.concatenate([deg_ref[d]] * (feat // tile), axis=1)


def fold_kernel(keep_ref, came_ref, out_ref):
    out_ref[...] = keep_ref[...] + came_ref[...]


def fold(keep, came):
    return pl.pallas_call(
        fold_kernel,
        in_specs=[whole(pltpu.VMEM)] * 2,
        out_specs=whole(pltpu.VMEM),
        out_shape=jax.ShapeDtypeStruct(keep.shape, jnp.float32),
        compiler_params=pltpu.CompilerParams(vmem_limit_bytes=VMEM_BYTES),
        name="fold_sums",
    )(keep, came)


def early(a, tiles, masks):
    tile, feat = tiles[0].shape
    return pl.pallas_call(
        functools.partial(early_kernel, masks),
        in_specs=[whole(pltpu.VMEM)] * (1 + len(tiles)),
        out_specs=whole(pltpu.VMEM),
        out_shape=jax.ShapeDtypeStruct((a.shape[1], feat), jnp.float32),
        scratch_shapes=[pltpu.VMEM((len(tiles), 2 * tile, feat), jnp.bfloat16)],
        compiler_params=pltpu.CompilerParams(vmem_limit_bytes=VMEM_BYTES),
        name="early_products",
    )(a, *tiles)


def late(a, deg, acc, tiles, masks, n_row):
    tile, feat = tiles[0].shape
    return pl.pallas_call(
        functools.partial(late_kernel, masks),
        in_specs=[whole(pltpu.VMEM)] * (3 + len(tiles)),
        out_specs=[whole(pltpu.VMEM)] * n_row,
        out_shape=[jax.ShapeDtypeStruct((tile + PAD, feat), jnp.float32)] * n_row,
        scratch_shapes=[pltpu.VMEM((len(tiles), 2 * tile, feat), jnp.bfloat16)],
        compiler_params=pltpu.CompilerParams(vmem_limit_bytes=VMEM_BYTES),
        name="late_products",
    )(a, deg, acc, *tiles)


def finish_kernel(own_ref, wn_ref, *refs):
    part_refs, out_ref = refs[:-1], refs[-1]
    tile, width = own_ref.shape
    total = part_refs[0][...]
    for ref in part_refs[1:]:
        total = total + ref[...]
    degree = jnp.broadcast_to(total[tile : tile + 1, 0:tile], (tile, tile)).T
    scale = 1.0 / jnp.maximum(degree, 1.0)
    scale = jnp.concatenate([scale] * (width // tile), axis=1)
    product = matmul_f32(total[0:tile, :], wn_ref[...])
    out_ref[...] = jnp.maximum(own_ref[...] + product * scale, 0.0)


def finish(own, wn, parts):
    return pl.pallas_call(
        finish_kernel,
        in_specs=[whole(pltpu.VMEM)] * (2 + len(parts)),
        out_specs=whole(pltpu.VMEM),
        out_shape=jax.ShapeDtypeStruct(own.shape, jnp.float32),
        compiler_params=pltpu.CompilerParams(vmem_limit_bytes=VMEM_BYTES),
        name="finish_rows",
    )(own, wn, *parts)


def after(value, *earlier):
    return lax.optimization_barrier((value, *earlier))[0]


def exchange(value, axis, mask):
    pairs = [(i, i ^ mask) for i in range(lax.axis_size(axis))]
    return lax.ppermute(value, axis, pairs)


def on_device(
    features, adj_tiles, tile_dst, tile_src, tile_count, self_weight, neighbor_weight, layer_bias
):
    n_row, n_col = lax.axis_size("row"), lax.axis_size("col")
    tile, maxt = adj_tiles.shape[-1], adj_tiles.shape[2]
    assert features.shape[0] == tile and maxt <= 256
    fill = -(2 * maxt + 1) % 128
    lists = jnp.concatenate(
        [tile_dst[0, 0], tile_src[0, 0], tile_count[0], jnp.zeros((fill,), jnp.int32)]
    )

    half = n_col // 2
    evens, odds = list(range(2, half, 2)), list(range(half - 1, 0, -2))
    tiles = {0: features}
    for mask in evens + [half, 1]:
        tiles[mask] = exchange(features, "col", mask)
    for mask in evens:
        tiles[mask + 1] = exchange(tiles[mask], "col", 1)
    first = list(tiles)
    far, lists = lax.optimization_barrier((tiles[half], lists))
    tiles[half] = far
    for mask in odds + evens:
        tiles[half + mask] = exchange(far, "col", mask)
    a, deg = combine(adj_tiles, lists, n_col, n_row)
    last = [mask for mask in tiles if mask not in first]
    acc = early(a, [tiles[mask] for mask in first], first)
    own = own_rows(features, self_weight, layer_bias)

    blocks = late(a, deg, acc, [tiles[mask] for mask in last], last, n_row)
    while len(blocks) > 4:
        bit = len(blocks) // 2
        blocks = [fold(blocks[m], exchange(blocks[m | bit], "row", bit)) for m in range(bit)]
    own_sum, beside, across, both = blocks
    across = exchange(fold(across, exchange(both, "row", 1)), "row", 2)
    beside = after(exchange(beside, "row", 1), across)
    return finish(own, neighbor_weight, [own_sum, beside, across])


def solution(mesh):
    placed = (
        P(("row", "col"), None),
        P("row", "col", None, None, None),
        P("row", "col", None),
        P("row", "col", None),
        P("row", "col"),
        P(),
        P(),
        P(),
    )
    return jax.shard_map(
        on_device, mesh=mesh, in_specs=placed, out_specs=P(("row", "col"), None), check_vma=False
    )
```

```python
import functools

import jax
import jax.numpy as jnp
from jax import lax
from jax.experimental import pallas as pl
from jax.experimental.pallas import tpu as pltpu
from jax.sharding import PartitionSpec as P

CHUNK = 8
PAD = 8
EAGER = 4
VMEM_BYTES = 32 * 1024 * 1024
COMBINE_VMEM = 51 * 1024 * 1024


def whole(space):
    return pl.BlockSpec(memory_space=space)


def split_bf16(value):
    high = value.astype(jnp.bfloat16)
    low = (value - high.astype(jnp.float32)).astype(jnp.bfloat16)
    return high, low


def matmul_f32(left, right):
    left_high, left_low = split_bf16(left)
    right_high, right_low = split_bf16(right)
    dot = functools.partial(jnp.dot, preferred_element_type=jnp.float32)
    return dot(left_high, right_high) + dot(left_high, right_low) + dot(left_low, right_high)


def combine_kernel(lists_hbm, adj_hbm, a_ref, deg_ref, lists_ref, held, list_sem, sems):
    maxt, tile = held.shape[0], held.shape[1]
    n_src, n_dst = a_ref.shape[0], a_ref.shape[1] // tile
    lists = pltpu.make_async_copy(lists_hbm, lists_ref, list_sem)
    lists.start()

    def block(index):
        part = pl.ds(index * CHUNK, CHUNK)
        return pltpu.make_async_copy(adj_hbm.at[0, 0, part], held.at[part], sems.at[index])

    chunks = maxt // CHUNK
    ahead = min(EAGER, chunks)
    for index in range(ahead):
        block(index).start()

    def clear(s, carry):
        a_ref[s] = jnp.zeros(a_ref.shape[1:], a_ref.dtype)
        return carry

    lax.fori_loop(0, n_src, clear, 0)
    lists.wait()
    count = lists_ref[2 * maxt]

    for index in range(ahead, chunks):

        @pl.when(index * CHUNK < count)
        def _():
            block(index).start()

    def add_tile(k, carry):
        rows = pl.ds(pl.multiple_of(lists_ref[k] * tile, tile), tile)
        source = lists_ref[maxt + k]
        a_ref[source, rows, :] = a_ref[source, rows, :] + held[k]
        return carry

    def add_block(index):
        block(index).wait()
        first = index * CHUNK
        lax.fori_loop(first, jnp.minimum(first + CHUNK, count), add_tile, 0)

    for index in range(chunks):
        if index < ahead:
            add_block(index)
        else:
            pl.when(index * CHUNK < count)(functools.partial(add_block, index))

    ones = jnp.ones((PAD, tile), jnp.bfloat16)

    def row_sums(d, carry):
        rows = pl.ds(pl.multiple_of(d * tile, tile), tile)
        joined = lax.fori_loop(
            1, n_src, lambda s, total: total + a_ref[s, rows, :], a_ref[0, rows, :]
        )
        deg_ref[d] = lax.dot_general(
            ones, joined, (((1,), (1,)), ((), ())), preferred_element_type=jnp.float32
        )
        return carry

    lax.fori_loop(0, n_dst, row_sums, 0)


def combine(adj, lists, n_src, n_dst):
    maxt, tile = adj.shape[2], adj.shape[3]
    return pl.pallas_call(
        combine_kernel,
        in_specs=[whole(pltpu.HBM)] * 2,
        out_specs=[whole(pltpu.VMEM)] * 2,
        out_shape=[
            jax.ShapeDtypeStruct((n_src, n_dst * tile, tile), jnp.bfloat16),
            jax.ShapeDtypeStruct((n_dst, PAD, tile), jnp.float32),
        ],
        scratch_shapes=[
            pltpu.SMEM(lists.shape, jnp.int32),
            pltpu.VMEM(adj.shape[2:], adj.dtype),
            pltpu.SemaphoreType.DMA(()),
            pltpu.SemaphoreType.DMA((maxt // CHUNK,)),
        ],
        compiler_params=pltpu.CompilerParams(vmem_limit_bytes=COMBINE_VMEM),
        name="combine_tiles",
    )(lists, adj)


def own_kernel(x_ref, ws_ref, b_ref, own_ref):
    own_ref[...] = matmul_f32(x_ref[...], ws_ref[...]) + b_ref[...][None, :]


def own_rows(x, ws, b):
    return pl.pallas_call(
        own_kernel,
        in_specs=[whole(pltpu.VMEM)] * 3,
        out_specs=whole(pltpu.VMEM),
        out_shape=jax.ShapeDtypeStruct((x.shape[0], ws.shape[1]), jnp.float32),
        compiler_params=pltpu.CompilerParams(vmem_limit_bytes=VMEM_BYTES),
        name="own_rows",
    )(x, ws, b)


def product_rows(a_ref, tile_refs, masks, halves, rows):
    total = None
    for index, mask in enumerate(masks):
        a = a_ref[lax.axis_index("col") ^ mask, rows, :]
        term = jnp.dot(
            jnp.concatenate([a, a], axis=1), halves[index], preferred_element_type=jnp.float32
        )
        total = term if total is None else total + term
    return total


def stack_halves(tile_refs, halves):
    tile = tile_refs[0].shape[0]
    for index, ref in enumerate(tile_refs):
        high, low = split_bf16(ref[...])
        halves[index, 0:tile, :] = high
        halves[index, tile:, :] = low


def early_kernel(masks, a_ref, *refs):
    tile_refs, acc_ref, halves = refs[: len(masks)], refs[-2], refs[-1]
    stack_halves(tile_refs, halves)
    height = min(acc_ref.shape[0], 512)

    def visit(step, carry):
        rows = pl.ds(pl.multiple_of(step * height, height), height)
        acc_ref[rows, :] = product_rows(a_ref, tile_refs, masks, halves, rows)
        return carry

    lax.fori_loop(0, acc_ref.shape[0] // height, visit, 0)


def late_kernel(masks, places, a_ref, deg_ref, acc_ref, *refs):
    tile_refs, out_refs, halves = refs[: len(masks)], refs[len(masks) : -1], refs[-1]
    tile, feat = tile_refs[0].shape
    stack_halves(tile_refs, halves)
    for place, out_ref in zip(places, out_refs):
        d = lax.axis_index("row") ^ place
        rows = pl.ds(pl.multiple_of(d * tile, tile), tile)
        out_ref[0:tile, :] = acc_ref[rows, :] + product_rows(
            a_ref, tile_refs, masks, halves, rows
        )
        out_ref[tile:, :] = jnp.concatenate([deg_ref[d]] * (feat // tile), axis=1)


def fold_kernel(keep_ref, came_ref, out_ref):
    out_ref[...] = keep_ref[...] + came_ref[...]


def fold(keep, came):
    return pl.pallas_call(
        fold_kernel,
        in_specs=[whole(pltpu.VMEM)] * 2,
        out_specs=whole(pltpu.VMEM),
        out_shape=jax.ShapeDtypeStruct(keep.shape, jnp.float32),
        compiler_params=pltpu.CompilerParams(vmem_limit_bytes=VMEM_BYTES),
        name="fold_sums",
    )(keep, came)


def early(a, tiles, masks):
    tile, feat = tiles[0].shape
    return pl.pallas_call(
        functools.partial(early_kernel, masks),
        in_specs=[whole(pltpu.VMEM)] * (1 + len(tiles)),
        out_specs=whole(pltpu.VMEM),
        out_shape=jax.ShapeDtypeStruct((a.shape[1], feat), jnp.float32),
        scratch_shapes=[pltpu.VMEM((len(tiles), 2 * tile, feat), jnp.bfloat16)],
        compiler_params=pltpu.CompilerParams(vmem_limit_bytes=VMEM_BYTES),
        name="early_products",
    )(a, *tiles)


def late(a, deg, acc, tiles, masks, places):
    tile, feat = tiles[0].shape
    return pl.pallas_call(
        functools.partial(late_kernel, masks, places),
        in_specs=[whole(pltpu.VMEM)] * (3 + len(tiles)),
        out_specs=[whole(pltpu.VMEM)] * len(places),
        out_shape=[jax.ShapeDtypeStruct((tile + PAD, feat), jnp.float32)] * len(places),
        scratch_shapes=[pltpu.VMEM((len(tiles), 2 * tile, feat), jnp.bfloat16)],
        compiler_params=pltpu.CompilerParams(vmem_limit_bytes=VMEM_BYTES),
        name="late_products",
    )(a, deg, acc, *tiles)


def finish_kernel(own_ref, wn_ref, *refs):
    part_refs, out_ref = refs[:-1], refs[-1]
    tile, width = own_ref.shape
    total = part_refs[0][...]
    for ref in part_refs[1:]:
        total = total + ref[...]
    degree = jnp.broadcast_to(total[tile : tile + 1, 0:tile], (tile, tile)).T
    scale = 1.0 / jnp.maximum(degree, 1.0)
    scale = jnp.concatenate([scale] * (width // tile), axis=1)
    product = matmul_f32(total[0:tile, :], wn_ref[...])
    out_ref[...] = jnp.maximum(own_ref[...] + product * scale, 0.0)


def finish(own, wn, parts):
    return pl.pallas_call(
        finish_kernel,
        in_specs=[whole(pltpu.VMEM)] * (2 + len(parts)),
        out_specs=whole(pltpu.VMEM),
        out_shape=jax.ShapeDtypeStruct(own.shape, jnp.float32),
        compiler_params=pltpu.CompilerParams(vmem_limit_bytes=VMEM_BYTES),
        name="finish_rows",
    )(own, wn, *parts)


def after(value, *earlier):
    return lax.optimization_barrier((value, *earlier))[0]


def exchange(value, axis, mask):
    pairs = [(i, i ^ mask) for i in range(lax.axis_size(axis))]
    return lax.ppermute(value, axis, pairs)


def on_device(
    features, adj_tiles, tile_dst, tile_src, tile_count, self_weight, neighbor_weight, layer_bias
):
    n_row, n_col = lax.axis_size("row"), lax.axis_size("col")
    tile, maxt = adj_tiles.shape[-1], adj_tiles.shape[2]
    assert features.shape[0] == tile and maxt <= 256
    fill = -(2 * maxt + 1) % 128
    lists = jnp.concatenate(
        [tile_dst[0, 0], tile_src[0, 0], tile_count[0], jnp.zeros((fill,), jnp.int32)]
    )

    half = n_col // 2
    evens, odds = list(range(2, half, 2)), list(range(half - 1, 0, -2))
    tiles = {0: features}
    for mask in evens + [half, 1]:
        tiles[mask] = exchange(features, "col", mask)
    for mask in evens:
        tiles[mask + 1] = exchange(tiles[mask], "col", 1)
    first = list(tiles)
    far, lists = lax.optimization_barrier((tiles[half], lists))
    tiles[half] = far
    for mask in odds + evens:
        tiles[half + mask] = exchange(far, "col", mask)
    a, deg = combine(adj_tiles, lists, n_col, n_row)
    last = [mask for mask in tiles if mask not in first]
    acc = early(a, [tiles[mask] for mask in first], first)
    own = own_rows(features, self_weight, layer_bias)

    split = max(3, n_row // 2)
    groups = [range(split, n_row), range(split)]
    sent, kept = [late(a, deg, acc, [tiles[m] for m in last], last, g) for g in groups]
    blocks = list(kept) + list(sent)
    while len(blocks) > 4:
        bit = len(blocks) // 2
        blocks = [fold(blocks[m], exchange(blocks[m | bit], "row", bit)) for m in range(bit)]
    own_sum, beside, across, both = blocks
    across = exchange(fold(across, exchange(both, "row", 1)), "row", 2)
    beside = after(exchange(beside, "row", 1), across)
    return finish(own, neighbor_weight, [own_sum, beside, across])


def solution(mesh):
    placed = (
        P(("row", "col"), None),
        P("row", "col", None, None, None),
        P("row", "col", None),
        P("row", "col", None),
        P("row", "col"),
        P(),
        P(),
        P(),
    )
    return jax.shard_map(
        on_device, mesh=mesh, in_specs=placed, out_specs=P(("row", "col"), None), check_vma=False
    )
```

```python
import functools

import jax
import jax.numpy as jnp
from jax import lax
from jax.experimental import pallas as pl
from jax.experimental.pallas import tpu as pltpu
from jax.sharding import PartitionSpec as P

CHUNK = 8
PAD = 8
EAGER = 4
VMEM_BYTES = 32 * 1024 * 1024
COMBINE_VMEM = 51 * 1024 * 1024


def whole(space):
    return pl.BlockSpec(memory_space=space)


def split_bf16(value):
    high = value.astype(jnp.bfloat16)
    low = (value - high.astype(jnp.float32)).astype(jnp.bfloat16)
    return high, low


def matmul_f32(left, right):
    left_high, left_low = split_bf16(left)
    right_high, right_low = split_bf16(right)
    dot = functools.partial(jnp.dot, preferred_element_type=jnp.float32)
    return dot(left_high, right_high) + dot(left_high, right_low) + dot(left_low, right_high)


def combine_kernel(lists_hbm, adj_hbm, a_ref, deg_ref, lists_ref, held, list_sem, sems):
    maxt, tile = held.shape[0], held.shape[1]
    n_src, n_dst = a_ref.shape[0], a_ref.shape[1] // tile
    lists = pltpu.make_async_copy(lists_hbm, lists_ref, list_sem)
    lists.start()

    def block(index):
        part = pl.ds(index * CHUNK, CHUNK)
        return pltpu.make_async_copy(adj_hbm.at[0, 0, part], held.at[part], sems.at[index])

    chunks = maxt // CHUNK
    ahead = min(EAGER, chunks)
    for index in range(ahead):
        block(index).start()

    def clear(s, carry):
        a_ref[s] = jnp.zeros(a_ref.shape[1:], a_ref.dtype)
        return carry

    lax.fori_loop(0, n_src, clear, 0)
    lists.wait()
    count = lists_ref[2 * maxt]

    for index in range(ahead, chunks):

        @pl.when(index * CHUNK < count)
        def _():
            block(index).start()

    def add_tile(k, carry):
        rows = pl.ds(pl.multiple_of(lists_ref[k] * tile, tile), tile)
        source = lists_ref[maxt + k]
        a_ref[source, rows, :] = a_ref[source, rows, :] + held[k]
        return carry

    def add_block(index):
        block(index).wait()
        first = index * CHUNK
        lax.fori_loop(first, jnp.minimum(first + CHUNK, count), add_tile, 0)

    for index in range(chunks):
        if index < ahead:
            add_block(index)
        else:
            pl.when(index * CHUNK < count)(functools.partial(add_block, index))

    ones = jnp.ones((PAD, tile), jnp.bfloat16)

    def row_sums(d, carry):
        rows = pl.ds(pl.multiple_of(d * tile, tile), tile)
        joined = lax.fori_loop(
            1, n_src, lambda s, total: total + a_ref[s, rows, :], a_ref[0, rows, :]
        )
        deg_ref[d] = lax.dot_general(
            ones, joined, (((1,), (1,)), ((), ())), preferred_element_type=jnp.float32
        )
        return carry

    lax.fori_loop(0, n_dst, row_sums, 0)


def combine(adj, lists, n_src, n_dst):
    maxt, tile = adj.shape[2], adj.shape[3]
    return pl.pallas_call(
        combine_kernel,
        in_specs=[whole(pltpu.HBM)] * 2,
        out_specs=[whole(pltpu.VMEM)] * 2,
        out_shape=[
            jax.ShapeDtypeStruct((n_src, n_dst * tile, tile), jnp.bfloat16),
            jax.ShapeDtypeStruct((n_dst, PAD, tile), jnp.float32),
        ],
        scratch_shapes=[
            pltpu.SMEM(lists.shape, jnp.int32),
            pltpu.VMEM(adj.shape[2:], adj.dtype),
            pltpu.SemaphoreType.DMA(()),
            pltpu.SemaphoreType.DMA((maxt // CHUNK,)),
        ],
        compiler_params=pltpu.CompilerParams(vmem_limit_bytes=COMBINE_VMEM),
        name="combine_tiles",
    )(lists, adj)


def own_kernel(x_ref, ws_ref, b_ref, wn_ref, own_ref, high_ref, low_ref):
    own_ref[...] = matmul_f32(x_ref[...], ws_ref[...]) + b_ref[...][None, :]
    high_ref[...], low_ref[...] = split_bf16(wn_ref[...])


def own_rows(x, ws, b, wn):
    half = jax.ShapeDtypeStruct(wn.shape, jnp.bfloat16)
    return pl.pallas_call(
        own_kernel,
        in_specs=[whole(pltpu.VMEM)] * 4,
        out_specs=[whole(pltpu.VMEM)] * 3,
        out_shape=[jax.ShapeDtypeStruct((x.shape[0], ws.shape[1]), jnp.float32), half, half],
        compiler_params=pltpu.CompilerParams(vmem_limit_bytes=VMEM_BYTES),
        name="own_rows",
    )(x, ws, b, wn)


def product_rows(a_ref, tile_refs, masks, halves, rows):
    total = None
    for index, mask in enumerate(masks):
        a = a_ref[lax.axis_index("col") ^ mask, rows, :]
        term = jnp.dot(
            jnp.concatenate([a, a], axis=1), halves[index], preferred_element_type=jnp.float32
        )
        total = term if total is None else total + term
    return total


def stack_halves(tile_refs, halves):
    tile = tile_refs[0].shape[0]
    for index, ref in enumerate(tile_refs):
        high, low = split_bf16(ref[...])
        halves[index, 0:tile, :] = high
        halves[index, tile:, :] = low


def early_kernel(masks, a_ref, *refs):
    tile_refs, acc_ref, halves = refs[: len(masks)], refs[-2], refs[-1]
    stack_halves(tile_refs, halves)
    height = min(acc_ref.shape[0], 512)

    def visit(step, carry):
        rows = pl.ds(pl.multiple_of(step * height, height), height)
        acc_ref[rows, :] = product_rows(a_ref, tile_refs, masks, halves, rows)
        return carry

    lax.fori_loop(0, acc_ref.shape[0] // height, visit, 0)


def late_kernel(masks, places, a_ref, deg_ref, acc_ref, *refs):
    tile_refs, out_refs, halves = refs[: len(masks)], refs[len(masks) : -1], refs[-1]
    tile, feat = tile_refs[0].shape
    stack_halves(tile_refs, halves)
    for place, out_ref in zip(places, out_refs):
        d = lax.axis_index("row") ^ place
        rows = pl.ds(pl.multiple_of(d * tile, tile), tile)
        out_ref[0:tile, :] = acc_ref[rows, :] + product_rows(
            a_ref, tile_refs, masks, halves, rows
        )
        out_ref[tile:, :] = jnp.concatenate([deg_ref[d]] * (feat // tile), axis=1)


def fold_kernel(keep_ref, came_ref, out_ref):
    out_ref[...] = keep_ref[...] + came_ref[...]


def fold(keep, came):
    return pl.pallas_call(
        fold_kernel,
        in_specs=[whole(pltpu.VMEM)] * 2,
        out_specs=whole(pltpu.VMEM),
        out_shape=jax.ShapeDtypeStruct(keep.shape, jnp.float32),
        compiler_params=pltpu.CompilerParams(vmem_limit_bytes=VMEM_BYTES),
        name="fold_sums",
    )(keep, came)


def early(a, tiles, masks):
    tile, feat = tiles[0].shape
    return pl.pallas_call(
        functools.partial(early_kernel, masks),
        in_specs=[whole(pltpu.VMEM)] * (1 + len(tiles)),
        out_specs=whole(pltpu.VMEM),
        out_shape=jax.ShapeDtypeStruct((a.shape[1], feat), jnp.float32),
        scratch_shapes=[pltpu.VMEM((len(tiles), 2 * tile, feat), jnp.bfloat16)],
        compiler_params=pltpu.CompilerParams(vmem_limit_bytes=VMEM_BYTES),
        name="early_products",
    )(a, *tiles)


def late(a, deg, acc, tiles, masks, places):
    tile, feat = tiles[0].shape
    return pl.pallas_call(
        functools.partial(late_kernel, masks, places),
        in_specs=[whole(pltpu.VMEM)] * (3 + len(tiles)),
        out_specs=[whole(pltpu.VMEM)] * len(places),
        out_shape=[jax.ShapeDtypeStruct((tile + PAD, feat), jnp.float32)] * len(places),
        scratch_shapes=[pltpu.VMEM((len(tiles), 2 * tile, feat), jnp.bfloat16)],
        compiler_params=pltpu.CompilerParams(vmem_limit_bytes=VMEM_BYTES),
        name="late_products",
    )(a, deg, acc, *tiles)


def finish_kernel(own_ref, high_ref, low_ref, here_ref, came_ref, out_ref):
    tile, width = own_ref.shape
    total = here_ref[...] + came_ref[...]
    degree = jnp.broadcast_to(total[tile : tile + 1, 0:tile], (tile, tile)).T
    scale = 1.0 / jnp.maximum(degree, 1.0)
    scale = jnp.concatenate([scale] * (width // tile), axis=1)
    high, low = split_bf16(total[0:tile, :])
    dot = functools.partial(jnp.dot, preferred_element_type=jnp.float32)
    product = dot(high, high_ref[...]) + dot(high, low_ref[...]) + dot(low, high_ref[...])
    out_ref[...] = jnp.maximum(own_ref[...] + product * scale, 0.0)


def finish(own, high, low, here, came):
    return pl.pallas_call(
        finish_kernel,
        in_specs=[whole(pltpu.VMEM)] * 5,
        out_specs=whole(pltpu.VMEM),
        out_shape=jax.ShapeDtypeStruct(own.shape, jnp.float32),
        compiler_params=pltpu.CompilerParams(vmem_limit_bytes=VMEM_BYTES),
        name="finish_rows",
    )(own, high, low, here, came)


def after(value, *earlier):
    return lax.optimization_barrier((value, *earlier))[0]


def exchange(value, axis, mask):
    pairs = [(i, i ^ mask) for i in range(lax.axis_size(axis))]
    return lax.ppermute(value, axis, pairs)


def on_device(
    features, adj_tiles, tile_dst, tile_src, tile_count, self_weight, neighbor_weight, layer_bias
):
    n_row, n_col = lax.axis_size("row"), lax.axis_size("col")
    tile, maxt = adj_tiles.shape[-1], adj_tiles.shape[2]
    assert features.shape[0] == tile and maxt <= 256
    fill = -(2 * maxt + 1) % 128
    lists = jnp.concatenate(
        [tile_dst[0, 0], tile_src[0, 0], tile_count[0], jnp.zeros((fill,), jnp.int32)]
    )

    half = n_col // 2
    evens, odds = list(range(2, half, 2)), list(range(half - 1, 0, -2))
    tiles = {0: features}
    for mask in evens + [half, 1]:
        tiles[mask] = exchange(features, "col", mask)
    for mask in evens:
        tiles[mask + 1] = exchange(tiles[mask], "col", 1)
    first = list(tiles)
    far, lists = lax.optimization_barrier((tiles[half], lists))
    tiles[half] = far
    for mask in odds + evens:
        tiles[half + mask] = exchange(far, "col", mask)
    a, deg = combine(adj_tiles, lists, n_col, n_row)
    last = [mask for mask in tiles if mask not in first]
    acc = early(a, [tiles[mask] for mask in first], first)
    own, high, low = own_rows(features, self_weight, layer_bias, neighbor_weight)

    split = max(3, n_row // 2)
    groups = [range(split, n_row), range(split)]
    sent, kept = [late(a, deg, acc, [tiles[m] for m in last], last, g) for g in groups]
    blocks = list(kept) + list(sent)
    while len(blocks) > 4:
        bit = len(blocks) // 2
        blocks = [fold(blocks[m], exchange(blocks[m | bit], "row", bit)) for m in range(bit)]
    own_sum, beside, across, both = blocks
    across = exchange(fold(across, exchange(both, "row", 1)), "row", 2)
    here = fold(own_sum, exchange(beside, "row", 1))
    return finish(own, high, low, here, across)


def solution(mesh):
    placed = (
        P(("row", "col"), None),
        P("row", "col", None, None, None),
        P("row", "col", None),
        P("row", "col", None),
        P("row", "col"),
        P(),
        P(),
        P(),
    )
    return jax.shard_map(
        on_device, mesh=mesh, in_specs=placed, out_specs=P(("row", "col"), None), check_vma=False
    )
```

```python
import functools

import jax
import jax.numpy as jnp
from jax import lax
from jax.experimental import pallas as pl
from jax.experimental.pallas import tpu as pltpu
from jax.sharding import PartitionSpec as P

CHUNK = 8
PAD = 8
EAGER = 8
VMEM_BYTES = 32 * 1024 * 1024
COMBINE_VMEM = 51 * 1024 * 1024


def whole(space):
    return pl.BlockSpec(memory_space=space)


def split_bf16(value):
    high = value.astype(jnp.bfloat16)
    low = (value - high.astype(jnp.float32)).astype(jnp.bfloat16)
    return high, low


def matmul_f32(left, right):
    left_high, left_low = split_bf16(left)
    right_high, right_low = split_bf16(right)
    dot = functools.partial(jnp.dot, preferred_element_type=jnp.float32)
    return dot(left_high, right_high) + dot(left_high, right_low) + dot(left_low, right_high)


def combine_kernel(lists_hbm, adj_hbm, a_ref, deg_ref, lists_ref, held, list_sem, sems):
    maxt, tile = held.shape[0], held.shape[1]
    n_src, n_dst = a_ref.shape[0], a_ref.shape[1] // tile
    lists = pltpu.make_async_copy(lists_hbm, lists_ref, list_sem)
    lists.start()

    def block(index):
        part = pl.ds(index * CHUNK, CHUNK)
        return pltpu.make_async_copy(adj_hbm.at[0, 0, part], held.at[part], sems.at[index])

    chunks = maxt // CHUNK
    ahead = min(EAGER, chunks)
    for index in range(ahead):
        block(index).start()

    def clear(s, carry):
        a_ref[s] = jnp.zeros(a_ref.shape[1:], a_ref.dtype)
        return carry

    lax.fori_loop(0, n_src, clear, 0)
    lists.wait()
    count = lists_ref[2 * maxt]

    for index in range(ahead, chunks):

        @pl.when(index * CHUNK < count)
        def _():
            block(index).start()

    def add_tile(k, carry):
        rows = pl.ds(pl.multiple_of(lists_ref[k] * tile, tile), tile)
        source = lists_ref[maxt + k]
        a_ref[source, rows, :] = a_ref[source, rows, :] + held[k]
        return carry

    def add_block(index):
        block(index).wait()
        first = index * CHUNK
        lax.fori_loop(first, jnp.minimum(first + CHUNK, count), add_tile, 0)

    for index in range(chunks):
        if index < ahead:
            add_block(index)
        else:
            pl.when(index * CHUNK < count)(functools.partial(add_block, index))

    ones = jnp.ones((PAD, tile), jnp.bfloat16)

    def row_sums(d, carry):
        rows = pl.ds(pl.multiple_of(d * tile, tile), tile)
        joined = lax.fori_loop(
            1, n_src, lambda s, total: total + a_ref[s, rows, :], a_ref[0, rows, :]
        )
        deg_ref[d] = lax.dot_general(
            ones, joined, (((1,), (1,)), ((), ())), preferred_element_type=jnp.float32
        )
        return carry

    lax.fori_loop(0, n_dst, row_sums, 0)


def combine(adj, lists, n_src, n_dst):
    maxt, tile = adj.shape[2], adj.shape[3]
    return pl.pallas_call(
        combine_kernel,
        in_specs=[whole(pltpu.HBM)] * 2,
        out_specs=[whole(pltpu.VMEM)] * 2,
        out_shape=[
            jax.ShapeDtypeStruct((n_src, n_dst * tile, tile), jnp.bfloat16),
            jax.ShapeDtypeStruct((n_dst, PAD, tile), jnp.float32),
        ],
        scratch_shapes=[
            pltpu.SMEM(lists.shape, jnp.int32),
            pltpu.VMEM(adj.shape[2:], adj.dtype),
            pltpu.SemaphoreType.DMA(()),
            pltpu.SemaphoreType.DMA((maxt // CHUNK,)),
        ],
        compiler_params=pltpu.CompilerParams(vmem_limit_bytes=COMBINE_VMEM),
        name="combine_tiles",
    )(lists, adj)


def own_kernel(x_ref, ws_ref, b_ref, wn_ref, own_ref, high_ref, low_ref):
    own_ref[...] = matmul_f32(x_ref[...], ws_ref[...]) + b_ref[...][None, :]
    high_ref[...], low_ref[...] = split_bf16(wn_ref[...])


def own_rows(x, ws, b, wn):
    half = jax.ShapeDtypeStruct(wn.shape, jnp.bfloat16)
    return pl.pallas_call(
        own_kernel,
        in_specs=[whole(pltpu.VMEM)] * 4,
        out_specs=[whole(pltpu.VMEM)] * 3,
        out_shape=[jax.ShapeDtypeStruct((x.shape[0], ws.shape[1]), jnp.float32), half, half],
        compiler_params=pltpu.CompilerParams(vmem_limit_bytes=VMEM_BYTES),
        name="own_rows",
    )(x, ws, b, wn)


def product_rows(a_ref, tile_refs, masks, halves, rows):
    total = None
    for index, mask in enumerate(masks):
        a = a_ref[lax.axis_index("col") ^ mask, rows, :]
        term = jnp.dot(
            jnp.concatenate([a, a], axis=1), halves[index], preferred_element_type=jnp.float32
        )
        total = term if total is None else total + term
    return total


def stack_halves(tile_refs, halves):
    tile = tile_refs[0].shape[0]
    for index, ref in enumerate(tile_refs):
        high, low = split_bf16(ref[...])
        halves[index, 0:tile, :] = high
        halves[index, tile:, :] = low


def early_kernel(masks, a_ref, *refs):
    tile_refs, acc_ref, halves = refs[: len(masks)], refs[-2], refs[-1]
    stack_halves(tile_refs, halves)
    height = min(acc_ref.shape[0], 512)

    def visit(step, carry):
        rows = pl.ds(pl.multiple_of(step * height, height), height)
        acc_ref[rows, :] = product_rows(a_ref, tile_refs, masks, halves, rows)
        return carry

    lax.fori_loop(0, acc_ref.shape[0] // height, visit, 0)


def late_kernel(masks, places, a_ref, deg_ref, acc_ref, *refs):
    tile_refs, out_refs, halves = refs[: len(masks)], refs[len(masks) : -1], refs[-1]
    tile, feat = tile_refs[0].shape
    stack_halves(tile_refs, halves)
    for place, out_ref in zip(places, out_refs):
        d = lax.axis_index("row") ^ place
        rows = pl.ds(pl.multiple_of(d * tile, tile), tile)
        out_ref[0:tile, :] = acc_ref[rows, :] + product_rows(
            a_ref, tile_refs, masks, halves, rows
        )
        out_ref[tile:, :] = jnp.concatenate([deg_ref[d]] * (feat // tile), axis=1)


def fold_kernel(keep_ref, came_ref, out_ref):
    out_ref[...] = keep_ref[...] + came_ref[...]


def fold(keep, came):
    return pl.pallas_call(
        fold_kernel,
        in_specs=[whole(pltpu.VMEM)] * 2,
        out_specs=whole(pltpu.VMEM),
        out_shape=jax.ShapeDtypeStruct(keep.shape, jnp.float32),
        compiler_params=pltpu.CompilerParams(vmem_limit_bytes=VMEM_BYTES),
        name="fold_sums",
    )(keep, came)


def early(a, tiles, masks):
    tile, feat = tiles[0].shape
    return pl.pallas_call(
        functools.partial(early_kernel, masks),
        in_specs=[whole(pltpu.VMEM)] * (1 + len(tiles)),
        out_specs=whole(pltpu.VMEM),
        out_shape=jax.ShapeDtypeStruct((a.shape[1], feat), jnp.float32),
        scratch_shapes=[pltpu.VMEM((len(tiles), 2 * tile, feat), jnp.bfloat16)],
        compiler_params=pltpu.CompilerParams(vmem_limit_bytes=VMEM_BYTES),
        name="early_products",
    )(a, *tiles)


def late(a, deg, acc, tiles, masks, places):
    tile, feat = tiles[0].shape
    return pl.pallas_call(
        functools.partial(late_kernel, masks, places),
        in_specs=[whole(pltpu.VMEM)] * (3 + len(tiles)),
        out_specs=[whole(pltpu.VMEM)] * len(places),
        out_shape=[jax.ShapeDtypeStruct((tile + PAD, feat), jnp.float32)] * len(places),
        scratch_shapes=[pltpu.VMEM((len(tiles), 2 * tile, feat), jnp.bfloat16)],
        compiler_params=pltpu.CompilerParams(vmem_limit_bytes=VMEM_BYTES),
        name="late_products",
    )(a, deg, acc, *tiles)


def finish_kernel(own_ref, high_ref, low_ref, here_ref, came_ref, out_ref):
    tile, width = own_ref.shape
    total = here_ref[...] + came_ref[...]
    degree = jnp.broadcast_to(total[tile : tile + 1, 0:tile], (tile, tile)).T
    scale = 1.0 / jnp.maximum(degree, 1.0)
    scale = jnp.concatenate([scale] * (width // tile), axis=1)
    high, low = split_bf16(total[0:tile, :])
    dot = functools.partial(jnp.dot, preferred_element_type=jnp.float32)
    product = dot(high, high_ref[...]) + dot(high, low_ref[...]) + dot(low, high_ref[...])
    out_ref[...] = jnp.maximum(own_ref[...] + product * scale, 0.0)


def finish(own, high, low, here, came):
    return pl.pallas_call(
        finish_kernel,
        in_specs=[whole(pltpu.VMEM)] * 5,
        out_specs=whole(pltpu.VMEM),
        out_shape=jax.ShapeDtypeStruct(own.shape, jnp.float32),
        compiler_params=pltpu.CompilerParams(vmem_limit_bytes=VMEM_BYTES),
        name="finish_rows",
    )(own, high, low, here, came)


def after(value, *earlier):
    return lax.optimization_barrier((value, *earlier))[0]


def exchange(value, axis, mask):
    pairs = [(i, i ^ mask) for i in range(lax.axis_size(axis))]
    return lax.ppermute(value, axis, pairs)


def on_device(
    features, adj_tiles, tile_dst, tile_src, tile_count, self_weight, neighbor_weight, layer_bias
):
    n_row, n_col = lax.axis_size("row"), lax.axis_size("col")
    tile, maxt = adj_tiles.shape[-1], adj_tiles.shape[2]
    assert features.shape[0] == tile and maxt <= 256
    fill = -(2 * maxt + 1) % 128
    lists = jnp.concatenate(
        [tile_dst[0, 0], tile_src[0, 0], tile_count[0], jnp.zeros((fill,), jnp.int32)]
    )

    half = n_col // 2
    evens, odds = list(range(2, half, 2)), list(range(half - 1, 0, -2))
    tiles = {0: features}
    for mask in evens + [half, 1]:
        tiles[mask] = exchange(features, "col", mask)
    for mask in evens:
        tiles[mask + 1] = exchange(tiles[mask], "col", 1)
    first = list(tiles)
    far, lists = lax.optimization_barrier((tiles[half], lists))
    tiles[half] = far
    for mask in odds + evens:
        tiles[half + mask] = exchange(far, "col", mask)
    a, deg = combine(adj_tiles, lists, n_col, n_row)
    last = [mask for mask in tiles if mask not in first]
    acc = early(a, [tiles[mask] for mask in first], first)
    own, high, low = own_rows(features, self_weight, layer_bias, neighbor_weight)

    split = max(3, n_row // 2)
    groups = [range(split, n_row), range(split)]
    sent, kept = [late(a, deg, acc, [tiles[m] for m in last], last, g) for g in groups]
    blocks = list(kept) + list(sent)
    while len(blocks) > 4:
        bit = len(blocks) // 2
        blocks = [fold(blocks[m], exchange(blocks[m | bit], "row", bit)) for m in range(bit)]
    own_sum, beside, across, both = blocks
    across = exchange(fold(across, exchange(both, "row", 1)), "row", 2)
    here = fold(own_sum, exchange(beside, "row", 1))
    return finish(own, high, low, here, across)


def solution(mesh):
    placed = (
        P(("row", "col"), None),
        P("row", "col", None, None, None),
        P("row", "col", None),
        P("row", "col", None),
        P("row", "col"),
        P(),
        P(),
        P(),
    )
    return jax.shard_map(
        on_device, mesh=mesh, in_specs=placed, out_specs=P(("row", "col"), None), check_vma=False
    )
```
